256 devices in a mesh: cond: 2 (over x_hi), gx: 8 (over z), gy: 16 (over x_lo, y, core).
Axes of the slice: x: 4 (x_hi: 2, x_lo: 2; x = x_hi * 2 + x_lo), y: 4, z: 8, core: 2. Of those that a mesh axis runs over, the one named last changes fastest.
Arguments:
- psi_old: float32 [64, 4, 6, 8192], P('gx', 'cond', None, 'gy'), may hold values from -6 to 6
- objective_grad: float32 [64, 4, 6, 8192], P('gx', 'cond', None, 'gy'), may hold values from -6 to 6
- near_upper: float32 [64, 4, 6, 6, 8192], P('gx', 'cond', None, None, 'gy'), may hold values from -1 to 0.06
- far_upper: float32 [64, 4, 6, 6, 8192], P('gx', 'cond', None, None, 'gy'), may hold values from -1 to 0.03
- inverse_diag: float32 [64, 4, 6, 6, 8192], P('gx', 'cond', None, None, 'gy'), may hold values from -0.06 to 1
- near_lower: float32 [64, 4, 6, 6, 8192], P('gx', 'cond', None, None, 'gy'), may hold values from -1 to 0.06
- far_lower: float32 [64, 4, 6, 6, 8192], P('gx', 'cond', None, None, 'gy'), may hold values from -1 to 0.03
- y_inverse: float32 [64, 4, 6, 6, 8192], P('gx', 'cond', None, None, 'gy'), may hold values from -0.1 to 1.5
- z_inverse: float32 [4, 6, 32, 32], P('cond'), may hold values from -1 to 1
- sens_terms: float32 [64, 4, 3, 6, 8192], P('gx', 'cond', None, None, 'gy'), may hold values from -1.25 to 1.25
- wall_mask: int32 [64, 8192], P('gx', 'gy'), may hold values 0 or 1
- cond_index: int32 [4], P('cond'), may hold values from 0 to 7
- weight_table: float32 [8], replicated, may hold values from 0.5 to 2
Outputs:
- psi_new: float32 [64, 4, 6, 8192], P('gx', 'cond', None, 'gy')
- mesh_sens: float32 [64, 3, 8192], P('gx', None, 'gy')
The draws below stay inside these ranges and needn't reach their ends.
All inputs are finite; a program needn't handle non-finite values. No bound on the sum of `wall_mask` on one device may be relied on, other than what follows from the above.
Results may differ from the reference program's by a relative error of at most 0.0001.
Values sent between devices are 32-bit elements; how exact they have to be, the bound alone decides.
A program may use at most 128 MiB of HBM per device.

```python
import math
import jax
import jax.numpy as jnp
from jax import lax

NV = 6
NZ = 32
ITERS = 2
NPOINTS = 8
NCOND = 4
STREAM_CELLS = 64
NY = 256
NYZ = 8192


def coupling(key):
    keys = jax.random.split(key, 8)
    rate_shape = (1, NCOND, NV, 1, NYZ)
    cell_shape = (STREAM_CELLS, NCOND, NV, 1, NYZ)
    full_shape = (STREAM_CELLS, NCOND, NV, NV, NYZ)
    slow_share = 0.5
    picked = jax.random.uniform(keys[0], rate_shape) < slow_share
    slow_low = 0.2 ** (1.0 / STREAM_CELLS)
    slow_high = 0.5 ** (1.0 / STREAM_CELLS)
    slow = slow_low + (slow_high - slow_low) * jax.random.uniform(keys[1], rate_shape)
    fast = jnp.exp(-jax.random.uniform(keys[2], rate_shape, minval=1.0 / 40.0, maxval=1.0 / 20.0))
    growth_rate = jnp.where(picked, slow, fast)
    coarse_guess = jax.random.uniform(keys[3], cell_shape, minval=0.985, maxval=1.0)
    spots = jax.random.randint(keys[4], (3,), 0, STREAM_CELLS)
    impact_hit = jnp.any(jnp.arange(STREAM_CELLS)[:, None] == spots[None, :], axis=1)
    sudden_jump = jnp.where(impact_hit, 0.65, 1.0).reshape(STREAM_CELLS, 1, 1, 1, 1)
    falloff_factor = growth_rate * coarse_guess * sudden_jump
    share = jax.random.uniform(keys[5], cell_shape, minval=0.75, maxval=0.9)
    ident = jnp.eye(NV, dtype=jnp.float32).reshape(1, 1, NV, NV, 1)
    near = -falloff_factor * share * ident + jax.random.uniform(keys[6], full_shape, minval=-0.06, maxval=0.06) * (1.0 - ident)
    far = -falloff_factor * (1.0 - share) * ident + jax.random.uniform(keys[7], full_shape, minval=-0.03, maxval=0.03) * (1.0 - ident)
    return (near, far)


def dominant(key, lower, upper, spread):
    keys = jax.random.split(key, 2)
    ident = jnp.eye(NV, dtype=jnp.float32).reshape(1, 1, NV, NV, 1)
    diagonal = jax.random.uniform(keys[0], (STREAM_CELLS, NCOND, NV, 1, NYZ), minval=lower, maxval=upper)
    rest = jax.random.uniform(keys[1], (STREAM_CELLS, NCOND, NV, NV, NYZ), minval=-spread, maxval=spread)
    return diagonal * ident + rest * (1.0 - ident)


def draw_near_upper(key, part):
    return coupling(jax.random.fold_in(key, 11))[0]


def draw_far_upper(key, part):
    return coupling(jax.random.fold_in(key, 11))[1]


def draw_near_lower(key, part):
    return coupling(jax.random.fold_in(key, 23))[0]


def draw_far_lower(key, part):
    return coupling(jax.random.fold_in(key, 23))[1]


def draw_inverse_diag(key, part):
    return dominant(jax.random.fold_in(key, 37), 0.8, 1.0, 0.06)


def draw_y_inverse(key, part):
    return dominant(jax.random.fold_in(key, 41), 0.5, 1.5, 0.1)


def set_ends(entries, rng, smallest, largest):
    index_at = [jax.random.randint(jax.random.fold_in(rng, axis), (), 0, length) for axis, length in enumerate(entries.shape)]
    longest = entries.shape.index(max(entries.shape))
    beside = index_at[:longest] + [(index_at[longest] + 1) % entries.shape[longest]] + index_at[longest + 1:]
    return entries.at[tuple(index_at)].set(smallest).at[tuple(beside)].set(largest)


def level_of(key, shape, cuts, low, top_value):
    def one(position, shards_of):
        steps = jax.random.uniform(jax.random.fold_in(jax.random.fold_in(key, 6), position), (shards_of,), jnp.float32, low / len(cuts), top_value / len(cuts))
        return jnp.repeat(jnp.exp(steps), shape[position] // shards_of).reshape((-1,) + (1,) * (len(shape) - position - 1))

    level = one(*cuts[0])
    for cut in cuts[1:]:
        level = level * one(*cut)
    return level


def noise(rng, dims, deviation, most, cuts=(), kind=jnp.bfloat16):
    entries = deviation * jax.random.normal(rng, dims, jnp.float32)
    if cuts:
        entries = entries * level_of(rng, dims, cuts, -0.22, 0.18)
    return jnp.clip(entries, -most, most).astype(kind)


def setup_inputs(seed: int = 0) -> dict:
    streams_of = jax.random.split(jax.random.key(seed), 14)
    psi_old = noise(streams_of[0], (STREAM_CELLS, NCOND, NV, NYZ), 1.0, 6.0, ((0, 8), (1, 2), (3, 16)), jnp.float32)
    objective_grad = noise(streams_of[1], (STREAM_CELLS, NCOND, NV, NYZ), 1.0, 6.0, ((0, 8), (1, 2), (3, 16)), jnp.float32)
    near_upper = draw_near_upper(jax.random.fold_in(streams_of[13], 71), 0)
    far_upper = draw_far_upper(jax.random.fold_in(streams_of[13], 71), 0)
    inverse_diag = draw_inverse_diag(jax.random.fold_in(streams_of[13], 71), 0)
    near_lower = draw_near_lower(jax.random.fold_in(streams_of[13], 71), 0)
    far_lower = draw_far_lower(jax.random.fold_in(streams_of[13], 71), 0)
    y_inverse = draw_y_inverse(jax.random.fold_in(streams_of[13], 71), 0)
    z_inverse = noise(streams_of[8], (NCOND, NV, NZ, NZ), NZ ** -0.5, 1.0, ((0, 2),), jnp.float32)
    sens_terms = noise(streams_of[9], (STREAM_CELLS, NCOND, 3, NV, NYZ), (NV * NCOND) ** -0.5, 1.25, ((0, 8), (1, 2), (4, 16)), jnp.float32)
    wall_mask = set_ends((jax.random.randint(streams_of[10], (STREAM_CELLS, NYZ), 0, 8) < 1).astype(jnp.int32), jax.random.fold_in(streams_of[10], 1), 0, 1)
    cond_index = set_ends(jax.random.randint(streams_of[11], (NCOND,), 0, NPOINTS), jax.random.fold_in(streams_of[11], 1), 0, NPOINTS - 1).astype(jnp.int32)
    weight_table = jnp.clip(jnp.exp(jax.random.uniform(streams_of[12], (NPOINTS,), jnp.float32, math.log(0.5), math.log(2.0))), 0.5, 2.0)
    return {"psi_old": psi_old, "objective_grad": objective_grad, "near_upper": near_upper, "far_upper": far_upper, "inverse_diag": inverse_diag, "near_lower": near_lower, "far_lower": far_lower, "y_inverse": y_inverse, "z_inverse": z_inverse, "sens_terms": sens_terms, "wall_mask": wall_mask, "cond_index": cond_index, "weight_table": weight_table}


def apply_block(blocks, vector):
    return jnp.sum(blocks * vector[..., None, :, :], axis=-2)


def apply_transpose(blocks, vector):
    return jnp.sum(blocks * vector[..., :, None, :], axis=-3)


def upper_sweep(rhs, near, far, incoming):
    def step(carry, item):
        last, before = carry
        value, near_cell, far_cell = item
        now = value - apply_block(near_cell, last) - apply_block(far_cell, before)
        return (now, last), now
    carry, values = lax.scan(step, (incoming[0], incoming[1]), (rhs, near, far))
    return values


def lower_sweep(rhs, inverse, near, far, incoming):
    def step(carry, item):
        pending, partial_value = carry
        value, inverse_cell, near_cell, far_cell = item
        now = apply_transpose(inverse_cell, value - pending)
        return (partial_value + apply_transpose(near_cell, now), apply_transpose(far_cell, now)), now
    carry, values = lax.scan(step, (incoming[0], incoming[1]), (rhs, inverse, near, far), reverse=True)
    return values


def reference(psi_old, objective_grad, near_upper, far_upper, inverse_diag, near_lower, far_lower, y_inverse, z_inverse, sens_terms, wall_mask, cond_index, weight_table):
    keep = (1.0 - wall_mask.astype(jnp.float32))[:, None, None, :]
    psi = psi_old
    zeros = jnp.zeros((2,) + psi_old.shape[1:], jnp.float32)
    for step in range(ITERS):
        grid = psi.reshape(STREAM_CELLS, NCOND, NV, NY, NZ)
        padded = jnp.pad(grid, ((1, 1), (0, 0), (0, 0), (1, 1), (0, 0)))
        beside_all = padded[2:, :, :, 1:-1] + padded[:-2, :, :, 1:-1] + padded[1:-1, :, :, 2:] + padded[1:-1, :, :, :-2]
        rhs = objective_grad + 0.5 * beside_all.reshape(psi.shape) - 2.0 * psi
        zres = jnp.einsum("icvjq,cvqk->icvjk", rhs.reshape(STREAM_CELLS, NCOND, NV, NY, NZ), z_inverse, precision=lax.Precision.HIGHEST).reshape(psi.shape)
        yres = apply_transpose(y_inverse, zres)
        upper = upper_sweep(yres, near_upper, far_upper, zeros)
        lower = lower_sweep(upper, inverse_diag, near_lower, far_lower, zeros)
        psi = (psi + 0.05 * lower) * keep
    onehot = (cond_index[:, None] == jnp.arange(NPOINTS)[None, :]).astype(jnp.float32)
    weights = jnp.sum(onehot * weight_table[None, :], axis=1)
    sens = jnp.einsum("icvl,icmvl->iml", psi * weights[None, :, None, None], sens_terms, precision=lax.Precision.HIGHEST)
    return psi, sens
```

```python
import functools

import jax
import jax.numpy as jnp
from jax import lax
from jax.experimental import pallas as pl
from jax.experimental.pallas import tpu as pltpu
from jax.sharding import PartitionSpec as P

MESH = pl.DeviceIdType.MESH
F32 = jnp.float32
BF16 = jnp.bfloat16
NX = 8
ORDER = (4, 3, 5, 2, 6, 1, 7)


def pack(x):
    n = x.ndim
    y = jnp.transpose(x, (0,) + tuple(range(2, n - 1)) + (1, n - 1))
    s = y.shape[:-2]
    y = jnp.swapaxes(y.reshape(s + (2, 4, 128)), -3, -2)
    return y.reshape(s + (8, 128))


def unpack(y):
    s = y.shape[:-2]
    y = jnp.swapaxes(y.reshape(s + (4, 2, 128)), -3, -2).reshape(s + (2, 512))
    n = y.ndim
    return jnp.transpose(y, (0, n - 2) + tuple(range(1, n - 2)) + (n - 1,))


def kernel(
    psi_h, grad_h, nu_h, fu_h, inv_h, nl_h, fl_h, yi_h, zi_h, sens_h, mask_h, ci, wt,
    psi_o, ms_o,
    grad, nu, fu, inv, nl, fl, yi, zi, sens, mask,
    psi, hj, keep, weights, xs, zs, up, p0, og, ogr, own, ef,
    resp, pr_e, pr_f, st_n, st_q, diff, m_r, n_r, q_r, t2, t4, s2, s4, rolled, part_o, part_r,
    load_sem, bulk_s, bulk_r, small_s, small_r, halo_s, halo_r, own_sem, sum_sem,
):
    k = lax.axis_index("gx")
    g = lax.axis_index("gy")
    cond = lax.axis_index("cond")
    last_g = lax.axis_size("gy") - 1
    sub = lax.broadcasted_iota(jnp.int32, (8, 128), 0)
    lane = lax.broadcasted_iota(jnp.int32, (8, 128), 1)

    loads = {}
    for n, (name, src, dst) in enumerate((
        ("psi", psi_h, psi.at[0, 1:9]), ("nu", nu_h, nu), ("fu", fu_h, fu), ("inv", inv_h, inv),
        ("nl", nl_h, nl), ("fl", fl_h, fl), ("zi", zi_h, zi), ("grad", grad_h, grad),
        ("yi", yi_h, yi), ("mask", mask_h, mask), ("sens", sens_h, sens),
    )):
        loads[name] = pltpu.make_async_copy(src, dst, load_sem.at[n])
        loads[name].start()

    zero = jnp.zeros((8, 128), F32)
    one = jnp.ones((8, 128), F32)
    for it in range(2):
        psi[it, 0] = jnp.zeros((6, 8, 128), F32)
        psi[it, 9] = jnp.zeros((6, 8, 128), F32)

    def clear(i, _):
        hj[i] = jnp.zeros((2, 6, 8, 128), F32)
        return 0

    lax.fori_loop(0, 16, clear, 0)

    def clear_matrix(i, _):
        m_r[i] = jnp.zeros((12, 8, 128), F32)
        n_r[i] = jnp.zeros((12, 8, 128), F32)
        q_r[i] = jnp.zeros((12, 8, 128), F32)
        return 0

    lax.fori_loop(0, 12, clear_matrix, 0)
    for s in range(2):
        for v in range(6):
            for q in range(12):
                unit = one if q == 6 * s + v else zero
                resp[s, v, q] = unit
                st_n[s, v, q] = unit
                st_q[s, v, q] = zero

    barrier = pltpu.get_barrier_semaphore()
    for d in range(1, NX):
        pl.semaphore_signal(barrier, inc=1, device_id={"gx": lax.rem(k + d, NX)}, device_id_type=MESH)
    pl.semaphore_signal(barrier, inc=1, device_id={"cond": 1 - cond}, device_id_type=MESH)

    @pl.when(g > 0)
    def _():
        pl.semaphore_signal(barrier, inc=1, device_id={"gy": g - 1}, device_id_type=MESH)

    @pl.when(g < last_g)
    def _():
        pl.semaphore_signal(barrier, inc=1, device_id={"gy": g + 1}, device_id_type=MESH)

    neighbours = jnp.where(g > 0, 1, 0) + jnp.where(g < last_g, 1, 0)
    pl.semaphore_wait(barrier, NX + neighbours)

    def halo_copy(it, n):
        if n == 0:
            src, dst, to = psi.at[it, 8], psi.at[it, 0], {"gx": lax.rem(k + 1, NX)}
        elif n == 1:
            src, dst, to = psi.at[it, 1], psi.at[it, 9], {"gx": lax.rem(k + NX - 1, NX)}
        elif n == 2:
            src, dst, to = psi.at[it, 1:9, :, 6:8], hj.at[pl.ds(it * 8, 8), 0, :, 0:2], {"gy": lax.rem(g + 1, last_g + 1)}
        else:
            src, dst, to = psi.at[it, 1:9, :, 0:2], hj.at[pl.ds(it * 8, 8), 1, :, 6:8], {"gy": lax.rem(g + last_g, last_g + 1)}
        return pltpu.make_async_remote_copy(
            src_ref=src, dst_ref=dst, send_sem=halo_s.at[it, n], recv_sem=halo_r.at[it, n],
            device_id=to, device_id_type=MESH)

    sends = (k < NX - 1, k > 0, g < last_g, g > 0)
    takes = (k > 0, k < NX - 1, g > 0, g < last_g)

    def halo_start(it, which):
        for n in which:
            @pl.when(sends[n])
            def _(n=n):
                halo_copy(it, n).start()

    def halo_wait(it):
        for n in range(4):
            @pl.when(takes[n])
            def _(n=n):
                halo_copy(it, n).wait_recv()

    def halo_drain(it):
        for n in range(4):
            @pl.when(sends[n])
            def _(n=n):
                halo_copy(it, n).wait_send()

    bulk = (
        (resp.at[8:10], m_r, lambda x: (x > 0) & (x < NX - 1), 1),
        (st_n, n_r, lambda x: (x > 0) & (x < NX - 1), -1),
        (st_q, q_r, lambda x: x > 0, -1),
    )

    def bulk_copy(n, d, source):
        src, dst, _, move = bulk[n]
        to = lax.rem(source + d, NX)
        row = lax.rem(source + NX + move, NX)
        return pltpu.make_async_remote_copy(
            src_ref=src.at[:, :, :, to], dst_ref=dst.reshape(2, 6, 12, 8, 128).at[:, :, :, row],
            send_sem=bulk_s.at[n, d], recv_sem=bulk_r.at[n, d],
            device_id={"gx": to}, device_id_type=MESH)

    def bulk_own(n):
        src, dst, _, move = bulk[n]
        row = lax.rem(k + NX + move, NX)
        return pltpu.make_async_copy(
            src.at[:, :, :, k], dst.reshape(2, 6, 12, 8, 128).at[:, :, :, row], own_sem.at[n])

    def bulk_start(n):
        @pl.when(bulk[n][2](k))
        def _():
            for d in ORDER:
                bulk_copy(n, d, k).start()
            bulk_own(n).start()

    def bulk_wait(n):
        for d in ORDER:
            source = lax.rem(k + NX - d, NX)

            @pl.when(bulk[n][2](source))
            def _(d=d, source=source):
                bulk_copy(n, d, source).wait_recv()

        @pl.when(bulk[n][2](k))
        def _():
            bulk_own(n).wait()

    def bulk_drain(n):
        @pl.when(bulk[n][2](k))
        def _():
            for d in ORDER:
                bulk_copy(n, d, k).wait_send()

    def small_copy(it, back, d, source):
        src, dst = (own, ef) if back else (og, ogr)
        to = lax.rem(source + d, NX)
        return pltpu.make_async_remote_copy(
            src_ref=src.at[it, :, to], dst_ref=dst.at[it, :, source],
            send_sem=small_s.at[2 * it + back, d], recv_sem=small_r.at[2 * it + back, d],
            device_id={"gx": to}, device_id_type=MESH)

    def small_exchange(it, back):
        src, dst = (own, ef) if back else (og, ogr)
        for d in ORDER:
            small_copy(it, back, d, k).start()
        mine = pltpu.make_async_copy(src.at[it, :, k], dst.at[it, :, k], own_sem.at[3 + 2 * it + back])
        mine.start()
        return mine

    def small_wait(it, back, mine):
        for d in ORDER:
            small_copy(it, back, d, lax.rem(k + NX - d, NX)).wait_recv()
        mine.wait()

    def small_drain(it, back):
        for d in ORDER:
            small_copy(it, back, d, k).wait_send()

    def upper_response(i, _):
        for w in range(0, 6, 2):
            acc = jnp.zeros((2, 12, 8, 128), F32)
            for v in range(6):
                acc += nu[i, w:w + 2, v][:, None] * resp[i + 1, v][None]
                acc += fu[i, w:w + 2, v][:, None] * resp[i, v][None]
            resp[i + 2, w:w + 2] = -acc
        return 0

    def lower_response(state, out, with_upper, t, _):
        i = NX - 1 - t
        for v in range(6):
            if with_upper:
                diff[v] = resp[i + 2, v] - state[0, v]
            else:
                diff[v] = -state[0, v]
        for w in range(0, 6, 2):
            acc = jnp.zeros((2, 12, 8, 128), F32)
            for v in range(6):
                acc += inv[i, v, w:w + 2][:, None] * diff[v][None]
            out[i, w:w + 2] = acc
        for w in range(0, 6, 2):
            near = state[1, w:w + 2]
            far = jnp.zeros((2, 12, 8, 128), F32)
            for v in range(6):
                p = out[i, v][None]
                near += nl[i, v, w:w + 2][:, None] * p
                far += fl[i, v, w:w + 2][:, None] * p
            state[0, w:w + 2] = near
            state[1, w:w + 2] = far
        return 0

    def local(it):
        halo_wait(it)
        for i in range(NX):
            here = psi[it, i + 1]
            down = pltpu.roll(here, 2, 1)
            down = jnp.where(sub < 2, hj[it * 8 + i, 0], down)
            down = pltpu.roll(jnp.where(lane >= 96, down, here), 32, 2)
            above = pltpu.roll(here, 6, 1)
            above = jnp.where(sub >= 6, hj[it * 8 + i, 1], above)
            above = pltpu.roll(jnp.where(lane < 32, above, here), 96, 2)
            beside = psi[it, i] + psi[it, i + 2] + down + above
            xs[:, i] = grad[i] + 0.5 * beside - 2.0 * here
        for v in range(6):
            x = xs[v].reshape(64, 128)
            hi = x.astype(BF16)
            lo = (x - hi.astype(F32)).astype(BF16)
            both = jnp.concatenate(
                [jnp.concatenate([hi, hi], axis=1), jnp.concatenate([lo, lo], axis=1)], axis=0)
            r = jnp.dot(both, weights[v], preferred_element_type=F32)
            r = (r[:64] + r[64:]).reshape(8, 8, 256)
            zs[v] = jnp.where(sub % 2 == 0, r[:, :, :128], r[:, :, 128:])
        last = jnp.zeros((6, 8, 128), F32)
        before = jnp.zeros((6, 8, 128), F32)
        for i in range(NX):
            now = jnp.zeros((6, 8, 128), F32)
            for v in range(6):
                now += yi[i, v] * zs[v, i]
            for v in range(6):
                now -= fu[i, :, v] * before[v]
            for v in range(6):
                now -= nu[i, :, v] * last[v]
            up[i] = now
            last, before = now, last
        og[it, 0:6] = before
        og[it, 6:12] = last
        pending = jnp.zeros((6, 8, 128), F32)
        partial = jnp.zeros((6, 8, 128), F32)
        for i in range(NX - 1, -1, -1):
            d = up[i] - pending
            p = jnp.zeros((6, 8, 128), F32)
            for v in range(6):
                p += inv[i, v] * d[v]
            p0[i] = p
            pending = partial
            partial = jnp.zeros((6, 8, 128), F32)
            for v in range(6):
                pending += nl[i, v] * p[v]
                partial += fl[i, v] * p[v]
        og[it, 12:18] = pending
        og[it, 18:24] = partial

    def product(dst, a, b, shift):
        def turn(q, _):
            rolled[q] = pltpu.roll(b[q], shift, 1)
            return 0

        lax.fori_loop(0, 12, turn, 0)

        def rows(m, _):
            acc = jnp.zeros((2, 12, 8, 128), F32)
            for q in range(12):
                acc += a[pl.ds(2 * m, 2), q][:, None] * rolled[q][None]
            dst[pl.ds(2 * m, 2)] = acc
            return 0

        lax.fori_loop(0, 6, rows, 0)

    def apply(x, a, by, shift):
        turned = pltpu.roll(by, shift, 1)
        for q in range(12):
            x = x + a[:, q] * turned[q]
        return x

    def owner(it):
        u = jnp.where(sub == 0, 0.0, pltpu.roll(ogr[it, 0:12], 1, 1))
        u = apply(u, m_r, u, 1)
        u = apply(u, t2, u, 2)
        u = apply(u, t4, u, 4)
        own[it, 0:12] = u
        w = jnp.where(sub == 7, 0.0, pltpu.roll(ogr[it, 12:24], 7, 1))
        w = apply(w, q_r, u, 7)
        w = apply(w, n_r, w, 7)
        w = apply(w, s2, w, 6)
        w = apply(w, s4, w, 4)
        own[it, 12:24] = w

    def solved(it, i):
        p = p0[i]
        for q in range(12):
            p += pr_e[i, :, q] * ef[it, q]
        for q in range(12):
            p += pr_f[i, :, q] * ef[it, 12 + q]
        return (psi[it, i + 1] + 0.05 * p) * keep[i]

    loads["psi"].wait()
    halo_start(0, range(4))
    loads["nu"].wait()
    loads["fu"].wait()
    lax.fori_loop(0, NX, upper_response, 0)
    bulk_start(0)
    loads["inv"].wait()
    loads["nl"].wait()
    loads["fl"].wait()
    lax.fori_loop(0, NX, functools.partial(lower_response, st_n, pr_f, False), 0)
    bulk_start(1)
    lax.fori_loop(0, NX, functools.partial(lower_response, st_q, pr_e, True), 0)
    bulk_start(2)

    loads["zi"].wait()
    z = zi[...].reshape(2 * 6 * 32, 32)
    z_hi = z.astype(BF16)
    z_lo = (z - z_hi.astype(F32)).astype(BF16)
    spread = (
        lax.broadcasted_iota(jnp.int32, (32, 128), 1) % 32 == lax.broadcasted_iota(jnp.int32, (32, 128), 0)
    ).astype(F32).astype(BF16)
    lane32 = lax.broadcasted_iota(jnp.int32, (32, 128), 1) // 32
    for half, part in enumerate((z_hi, z_lo)):
        tiled = jnp.dot(part, spread, preferred_element_type=F32)
        for c in range(2):
            for v in range(6):
                at = (c * 6 + v) * 32
                rows = tiled[at:at + 32]
                for b in range(4):
                    weights[v, half * 128 + b * 32:half * 128 + b * 32 + 32, c * 128:c * 128 + 128] = (
                        jnp.where(lane32 == b, rows, 0.0).astype(BF16))
    loads["mask"].wait()
    open_cells = 1.0 - mask[...].astype(F32)
    for i in range(NX):
        row = jnp.zeros((8, 128), F32)
        for j in range(4):
            row = jnp.where(sub // 2 == j, open_cells[i:i + 1, j * 128:j * 128 + 128], row)
        keep[i] = row

    loads["grad"].wait()
    loads["yi"].wait()
    local(0)
    mine = small_exchange(0, 0)
    bulk_wait(0)
    product(t2, m_r, m_r, 1)
    product(t4, t2, t2, 2)
    bulk_wait(1)
    product(s2, n_r, n_r, 7)
    product(s4, s2, s2, 6)
    bulk_wait(2)
    small_wait(0, 0, mine)
    owner(0)
    mine = small_exchange(0, 1)
    small_wait(0, 1, mine)
    for i in (7, 0):
        psi[1, i + 1] = solved(0, i)
    halo_start(1, (0, 1))
    for i in range(1, 7):
        psi[1, i + 1] = solved(0, i)
    halo_start(1, (2, 3))
    local(1)
    mine = small_exchange(1, 0)
    small_wait(1, 0, mine)
    owner(1)
    mine = small_exchange(1, 1)
    loads["sens"].wait()
    factor = []
    for c in range(2):
        value = 0.0
        for n in range(8):
            value = value + jnp.where(ci[c] == n, wt[n], 0.0)
        factor.append(value)
    weight = jnp.where(sub % 2 == 0, factor[0], factor[1])
    small_wait(1, 1, mine)
    tiles = [[jnp.zeros((8, 128), F32) for _ in range(4)] for _ in range(3)]
    for i in range(NX):
        new = solved(1, i)
        psi_o[i] = new
        new = new * weight
        for m in range(3):
            total = jnp.zeros((8, 128), F32)
            for v in range(6):
                total += new[v] * sens[i, m, v]
            total += pltpu.roll(total, 7, 0)
            for j in range(4):
                shift = (i - 2 * j) % 8
                turned = pltpu.roll(total, shift, 0) if shift else total
                tiles[m][j] = jnp.where(sub == i, turned, tiles[m][j])
    for m in range(3):
        for j in range(4):
            part_o[m, :, j * 128:j * 128 + 128] = tiles[m][j]
    across = pltpu.make_async_remote_copy(
        src_ref=part_o, dst_ref=part_r, send_sem=sum_sem.at[0], recv_sem=sum_sem.at[1],
        device_id={"cond": 1 - cond}, device_id_type=MESH)
    across.start()
    for n in range(3):
        bulk_drain(n)
    for it in range(2):
        halo_drain(it)
        small_drain(it, 0)
        small_drain(it, 1)
    across.wait()
    ms_o[...] = part_o[...] + part_r[...]


def on_device(
    psi_old, objective_grad, near_upper, far_upper, inverse_diag, near_lower, far_lower,
    y_inverse, z_inverse, sens_terms, wall_mask, cond_index, weight_table,
):
    cell = (8, 6, 8, 128)
    block = (8, 6, 6, 8, 128)
    matrix = (12, 12, 8, 128)
    vm = lambda *shape: pltpu.VMEM(shape, F32)
    dma = pltpu.SemaphoreType.DMA
    far = pl.BlockSpec(memory_space=pl.ANY)
    scalars = pl.BlockSpec(memory_space=pltpu.SMEM)
    near = pl.BlockSpec(memory_space=pltpu.VMEM)
    psi, sens = pl.pallas_call(
        kernel,
        name="adjoint",
        out_shape=(jax.ShapeDtypeStruct(cell, F32), jax.ShapeDtypeStruct((3, 8, 512), F32)),
        in_specs=[far] * 11 + [scalars] * 2,
        out_specs=(near, near),
        scratch_shapes=[
            vm(*cell), vm(*block), vm(*block), vm(*block), vm(*block), vm(*block), vm(*block),
            vm(2, 6, 32, 32), vm(8, 3, 6, 8, 128), pltpu.VMEM((8, 512), jnp.int32),
            vm(2, 10, 6, 8, 128), vm(16, 2, 6, 8, 128), vm(8, 8, 128), pltpu.VMEM((6, 256, 256), BF16),
            vm(6, 8, 8, 128), vm(6, 8, 8, 128), vm(*cell), vm(*cell),
            vm(2, 24, 8, 128), vm(2, 24, 8, 128), vm(2, 24, 8, 128), vm(2, 24, 8, 128),
            vm(10, 6, 12, 8, 128), vm(8, 6, 12, 8, 128), vm(8, 6, 12, 8, 128),
            vm(2, 6, 12, 8, 128), vm(2, 6, 12, 8, 128), vm(6, 12, 8, 128),
            vm(*matrix), vm(*matrix), vm(*matrix), vm(*matrix), vm(*matrix), vm(*matrix), vm(*matrix), vm(*matrix),
            vm(3, 8, 512), vm(3, 8, 512),
            dma((11,)), dma((3, 8)), dma((3, 8)), dma((4, 8)), dma((4, 8)), dma((2, 4)), dma((2, 4)),
            dma((7,)), dma((2,)),
        ],
        compiler_params=pltpu.CompilerParams(
            collective_id=0, has_side_effects=True, vmem_limit_bytes=58 * 2**20),
        cost_estimate=pl.CostEstimate(flops=10**8, bytes_accessed=9 * 10**6, transcendentals=0),
    )(
        pack(psi_old), pack(objective_grad), pack(near_upper), pack(far_upper), pack(inverse_diag),
        pack(near_lower), pack(far_lower), pack(y_inverse), z_inverse, pack(sens_terms),
        wall_mask, cond_index, weight_table,
    )
    return unpack(psi), jnp.transpose(sens, (1, 0, 2))


def solution(mesh):
    cell = P("gx", "cond", None, "gy")
    block = P("gx", "cond", None, None, "gy")
    placed = (
        cell, cell, block, block, block, block, block, block,
        P("cond", None, None, None), block, P("gx", "gy"), P("cond"), P(),
    )
    return jax.shard_map(
        on_device, mesh=mesh, in_specs=placed, out_specs=(cell, P("gx", None, "gy")), check_vma=False)
```

```python
import functools

import jax
import jax.numpy as jnp
from jax import lax
from jax.experimental import pallas as pl
from jax.experimental.pallas import tpu as pltpu
from jax.sharding import PartitionSpec as P

MESH = pl.DeviceIdType.MESH
F32 = jnp.float32
BF16 = jnp.bfloat16
NX = 8
ORDER = (4, 3, 5, 2, 6, 1, 7)


def pack(x):
    n = x.ndim
    y = jnp.transpose(x, (0,) + tuple(range(2, n - 1)) + (1, n - 1))
    s = y.shape[:-2]
    y = jnp.swapaxes(y.reshape(s + (2, 4, 128)), -3, -2)
    return y.reshape(s + (8, 128))


def unpack(y):
    s = y.shape[:-2]
    y = jnp.swapaxes(y.reshape(s + (4, 2, 128)), -3, -2).reshape(s + (2, 512))
    n = y.ndim
    return jnp.transpose(y, (0, n - 2) + tuple(range(1, n - 2)) + (n - 1,))


def kernel(
    psi_h, grad_h, nu_h, fu_h, inv_h, nl_h, fl_h, yi_h, zi_h, sens_h, mask_h, ci, wt,
    psi_o, ms_o,
    grad, nu, fu, inv, nl, fl, yi, zi, sens, mask,
    psi, hj, keep, weights, xs, zs, up, p0, og, ogr, own, ef,
    resp, pr_e, pr_f, st_n, st_q, diff, m_r, n_r, q_r, t2, t4, s2, s4, rolled, part_o, part_r,
    load_sem, bulk_s, bulk_r, small_s, small_r, halo_s, halo_r, own_sem, sum_sem,
):
    k = lax.axis_index("gx")
    g = lax.axis_index("gy")
    cond = lax.axis_index("cond")
    last_g = lax.axis_size("gy") - 1
    sub = lax.broadcasted_iota(jnp.int32, (8, 128), 0)
    lane = lax.broadcasted_iota(jnp.int32, (8, 128), 1)

    loads = {}
    for n, (name, src, dst) in enumerate((
        ("nu", nu_h, nu), ("fu", fu_h, fu), ("psi", psi_h, psi.at[0, 1:9]), ("inv", inv_h, inv),
        ("nl", nl_h, nl), ("fl", fl_h, fl), ("zi", zi_h, zi), ("grad", grad_h, grad),
        ("yi", yi_h, yi), ("mask", mask_h, mask), ("sens", sens_h, sens),
    )):
        loads[name] = pltpu.make_async_copy(src, dst, load_sem.at[n])
        if n < 3:
            loads[name].start()

    zero = jnp.zeros((8, 128), F32)
    one = jnp.ones((8, 128), F32)
    for it in range(2):
        psi[it, 0] = jnp.zeros((6, 8, 128), F32)
        psi[it, 9] = jnp.zeros((6, 8, 128), F32)

    def clear(i, _):
        hj[i] = jnp.zeros((2, 6, 8, 128), F32)
        return 0

    lax.fori_loop(0, 16, clear, 0)

    def clear_matrix(i, _):
        m_r[i] = jnp.zeros((12, 8, 128), F32)
        n_r[i] = jnp.zeros((12, 8, 128), F32)
        q_r[i] = jnp.zeros((12, 8, 128), F32)
        return 0

    lax.fori_loop(0, 12, clear_matrix, 0)

    barrier = pltpu.get_barrier_semaphore()
    for d in range(1, NX):
        pl.semaphore_signal(barrier, inc=1, device_id={"gx": lax.rem(k + d, NX)}, device_id_type=MESH)
    pl.semaphore_signal(barrier, inc=1, device_id={"cond": 1 - cond}, device_id_type=MESH)

    @pl.when(g > 0)
    def _():
        pl.semaphore_signal(barrier, inc=1, device_id={"gy": g - 1}, device_id_type=MESH)

    @pl.when(g < last_g)
    def _():
        pl.semaphore_signal(barrier, inc=1, device_id={"gy": g + 1}, device_id_type=MESH)

    def halo_copy(it, n):
        if n == 0:
            src, dst, to = psi.at[it, 8], psi.at[it, 0], {"gx": lax.rem(k + 1, NX)}
        elif n == 1:
            src, dst, to = psi.at[it, 1], psi.at[it, 9], {"gx": lax.rem(k + NX - 1, NX)}
        elif n == 2:
            src, dst, to = psi.at[it, 1:9, :, 6:8], hj.at[pl.ds(it * 8, 8), 0, :, 0:2], {"gy": lax.rem(g + 1, last_g + 1)}
        else:
            src, dst, to = psi.at[it, 1:9, :, 0:2], hj.at[pl.ds(it * 8, 8), 1, :, 6:8], {"gy": lax.rem(g + last_g, last_g + 1)}
        return pltpu.make_async_remote_copy(
            src_ref=src, dst_ref=dst, send_sem=halo_s.at[it, n], recv_sem=halo_r.at[it, n],
            device_id=to, device_id_type=MESH)

    sends = (k < NX - 1, k > 0, g < last_g, g > 0)
    takes = (k > 0, k < NX - 1, g > 0, g < last_g)

    def halo_start(it, which):
        for n in which:
            @pl.when(sends[n])
            def _(n=n):
                halo_copy(it, n).start()

    def halo_wait(it):
        for n in range(4):
            @pl.when(takes[n])
            def _(n=n):
                halo_copy(it, n).wait_recv()

    def halo_drain(it):
        for n in range(4):
            @pl.when(sends[n])
            def _(n=n):
                halo_copy(it, n).wait_send()

    bulk = (
        (resp.reshape(720, 8, 128).at[576:720], m_r, lambda x: (x > 0) & (x < NX - 1), 1, (0, 144), 0),
        (st_n.reshape(144, 8, 128), n_r, lambda x: (x > 0) & (x < NX - 1), -1, (0, 48, 96, 144), 1),
        (st_q.reshape(144, 8, 128), q_r, lambda x: x > 0, -1, (0, 48, 108, 144), 4),
    )

    def bulk_copy(n, d, source, part):
        src, dst, _, move, cuts, first = bulk[n]
        to = lax.rem(source + d, NX)
        row = lax.rem(source + NX + move, NX)
        span = slice(cuts[part], cuts[part + 1])
        return pltpu.make_async_remote_copy(
            src_ref=src.at[span, to], dst_ref=dst.reshape(144, 8, 128).at[span, row],
            send_sem=bulk_s.at[first + part, d], recv_sem=bulk_r.at[first + part, d],
            device_id={"gx": to}, device_id_type=MESH)

    def bulk_own(n):
        src, dst, _, move, _, _ = bulk[n]
        row = lax.rem(k + NX + move, NX)
        return pltpu.make_async_copy(src.at[:, k], dst.reshape(144, 8, 128).at[:, row], own_sem.at[n])

    def bulk_start(n, part=0):
        @pl.when(bulk[n][2](k))
        def _():
            for d in ORDER:
                bulk_copy(n, d, k, part).start()
            if part == 0:
                bulk_own(n).start()

    def bulk_wait(n):
        for part in range(len(bulk[n][4]) - 1):
            for d in ORDER:
                source = lax.rem(k + NX - d, NX)

                @pl.when(bulk[n][2](source))
                def _(d=d, source=source, part=part):
                    bulk_copy(n, d, source, part).wait_recv()

        @pl.when(bulk[n][2](k))
        def _():
            bulk_own(n).wait()

    def bulk_drain(n):
        @pl.when(bulk[n][2](k))
        def _():
            for part in range(len(bulk[n][4]) - 1):
                for d in ORDER:
                    bulk_copy(n, d, k, part).wait_send()

    small = ((0, 0, 0, 12), (0, 1, 0, 12), (0, 0, 12, 24), (0, 1, 12, 24), (1, 0, 0, 24), (1, 1, 0, 24))

    def small_copy(n, d, source):
        it, back, first, end = small[n]
        src, dst = (own, ef) if back else (og, ogr)
        to = lax.rem(source + d, NX)
        return pltpu.make_async_remote_copy(
            src_ref=src.at[it, first:end, to], dst_ref=dst.at[it, first:end, source],
            send_sem=small_s.at[n, d], recv_sem=small_r.at[n, d],
            device_id={"gx": to}, device_id_type=MESH)

    def small_own(n):
        it, back, first, end = small[n]
        src, dst = (own, ef) if back else (og, ogr)
        return pltpu.make_async_copy(src.at[it, first:end, k], dst.at[it, first:end, k], own_sem.at[3 + n])

    def small_start(n):
        for d in ORDER:
            small_copy(n, d, k).start()
        small_own(n).start()

    def small_wait(n):
        for d in ORDER:
            small_copy(n, d, lax.rem(k + NX - d, NX)).wait_recv()
        small_own(n).wait()

    def small_drain(n):
        for d in ORDER:
            small_copy(n, d, k).wait_send()

    def upper_response(i, _):
        for w in range(0, 6, 2):
            acc = jnp.zeros((2, 12, 8, 128), F32)
            for v in range(6):
                acc += nu[i, w:w + 2, v][:, None] * resp[i + 1, v][None]
                acc += fu[i, w:w + 2, v][:, None] * resp[i, v][None]
            resp[i + 2, w:w + 2] = -acc
        return 0

    def lower_response(state, out, with_upper, t, _):
        i = NX - 1 - t
        for v in range(6):
            if with_upper:
                diff[v] = resp[i + 2, v] - state[0, v]
            else:
                diff[v] = -state[0, v]
        for w in range(0, 6, 2):
            acc = jnp.zeros((2, 12, 8, 128), F32)
            for v in range(6):
                acc += inv[i, v, w:w + 2][:, None] * diff[v][None]
            out[i, w:w + 2] = acc
        for w in range(0, 6, 2):
            near = state[1, w:w + 2]
            far = jnp.zeros((2, 12, 8, 128), F32)
            for v in range(6):
                p = out[i, v][None]
                near += nl[i, v, w:w + 2][:, None] * p
                far += fl[i, v, w:w + 2][:, None] * p
            state[0, w:w + 2] = near
            state[1, w:w + 2] = far
        return 0

    def local(it):
        halo_wait(it)
        for i in range(NX):
            here = psi[it, i + 1]
            down = pltpu.roll(here, 2, 1)
            down = jnp.where(sub < 2, hj[it * 8 + i, 0], down)
            down = pltpu.roll(jnp.where(lane >= 96, down, here), 32, 2)
            above = pltpu.roll(here, 6, 1)
            above = jnp.where(sub >= 6, hj[it * 8 + i, 1], above)
            above = pltpu.roll(jnp.where(lane < 32, above, here), 96, 2)
            beside = psi[it, i] + psi[it, i + 2] + down + above
            xs[:, i] = grad[i] + 0.5 * beside - 2.0 * here
        for v in range(6):
            x = xs[v].reshape(64, 128)
            hi = x.astype(BF16)
            lo = (x - hi.astype(F32)).astype(BF16)
            both = jnp.concatenate(
                [jnp.concatenate([hi, hi], axis=1), jnp.concatenate([lo, lo], axis=1)], axis=0)
            r = jnp.dot(both, weights[v], preferred_element_type=F32)
            r = (r[:64] + r[64:]).reshape(8, 8, 256)
            zs[v] = jnp.where(sub % 2 == 0, r[:, :, :128], r[:, :, 128:])
        last = jnp.zeros((6, 8, 128), F32)
        before = jnp.zeros((6, 8, 128), F32)
        for i in range(NX):
            now = jnp.zeros((6, 8, 128), F32)
            for v in range(6):
                now += yi[i, v] * zs[v, i]
            for v in range(6):
                now -= fu[i, :, v] * before[v]
            for v in range(6):
                now -= nu[i, :, v] * last[v]
            up[i] = now
            last, before = now, last
        og[it, 0:6] = before
        og[it, 6:12] = last
        pending = jnp.zeros((6, 8, 128), F32)
        partial = jnp.zeros((6, 8, 128), F32)
        for i in range(NX - 1, -1, -1):
            d = up[i] - pending
            p = jnp.zeros((6, 8, 128), F32)
            for v in range(6):
                p += inv[i, v] * d[v]
            p0[i] = p
            pending = partial
            partial = jnp.zeros((6, 8, 128), F32)
            for v in range(6):
                pending += nl[i, v] * p[v]
                partial += fl[i, v] * p[v]
        og[it, 12:18] = pending
        og[it, 18:24] = partial

    def product(dst, a, b, shift):
        def turn(q, _):
            rolled[q] = pltpu.roll(b[q], shift, 1)
            return 0

        lax.fori_loop(0, 12, turn, 0)

        def rows(m, _):
            acc = jnp.zeros((2, 12, 8, 128), F32)
            for q in range(12):
                acc += a[pl.ds(2 * m, 2), q][:, None] * rolled[q][None]
            dst[pl.ds(2 * m, 2)] = acc
            return 0

        lax.fori_loop(0, 6, rows, 0)

    def apply(x, a, by, shift):
        turned = pltpu.roll(by, shift, 1)
        for q in range(12):
            x = x + a[:, q] * turned[q]
        return x

    def steps(x, a, shift):
        return lax.fori_loop(0, NX - 2, lambda _, y: apply(x, a, y, shift), x)

    def owner_upper(it):
        u = jnp.where(sub == 0, 0.0, pltpu.roll(ogr[it, 0:12], 1, 1))
        if it == 0:
            u = steps(u, m_r, 1)
        else:
            u = apply(u, m_r, u, 1)
            u = apply(u, t2, u, 2)
            u = apply(u, t4, u, 4)
        own[it, 0:12] = u
        return u

    def owner_lower(it, u):
        w = jnp.where(sub == 7, 0.0, pltpu.roll(ogr[it, 12:24], 7, 1))
        if it == 0:
            w = steps(w, n_r, 7)
        else:
            w = apply(w, q_r, u, 7)
            w = apply(w, n_r, w, 7)
            w = apply(w, s2, w, 6)
            w = apply(w, s4, w, 4)
        own[it, 12:24] = w

    def solved(it, i):
        p = p0[i]
        for q in range(12):
            p += pr_e[i, :, q] * ef[it, q]
        for q in range(12):
            p += pr_f[i, :, q] * ef[it, 12 + q]
        return (psi[it, i + 1] + 0.05 * p) * keep[i]

    for s in range(2):
        for v in range(6):
            for q in range(12):
                unit = one if q == 6 * s + v else zero
                resp[s, v, q] = unit
                st_n[s, v, q] = unit
                st_q[s, v, q] = zero

    loads["nu"].wait()
    loads["fu"].wait()
    for name in ("inv", "nl", "fl", "zi", "grad", "yi", "mask", "sens"):
        loads[name].start()
    lax.fori_loop(0, NX, upper_response, 0)
    loads["psi"].wait()
    neighbours = jnp.where(g > 0, 1, 0) + jnp.where(g < last_g, 1, 0)
    pl.semaphore_wait(barrier, NX + neighbours)
    halo_start(0, range(4))
    bulk_start(0)
    loads["inv"].wait()
    loads["nl"].wait()
    loads["fl"].wait()
    lax.fori_loop(0, NX, functools.partial(lower_response, st_n, pr_f, False), 0)
    lax.fori_loop(0, NX, functools.partial(lower_response, st_q, pr_e, True), 0)

    loads["zi"].wait()
    z = zi[...].reshape(2 * 6 * 32, 32)
    z_hi = z.astype(BF16)
    z_lo = (z - z_hi.astype(F32)).astype(BF16)
    spread = (
        lax.broadcasted_iota(jnp.int32, (32, 128), 1) % 32 == lax.broadcasted_iota(jnp.int32, (32, 128), 0)
    ).astype(F32).astype(BF16)
    lane32 = lax.broadcasted_iota(jnp.int32, (32, 128), 1) // 32
    for half, part in enumerate((z_hi, z_lo)):
        tiled = jnp.dot(part, spread, preferred_element_type=F32)
        for c in range(2):
            for v in range(6):
                at = (c * 6 + v) * 32
                rows = tiled[at:at + 32]
                for b in range(4):
                    weights[v, half * 128 + b * 32:half * 128 + b * 32 + 32, c * 128:c * 128 + 128] = (
                        jnp.where(lane32 == b, rows, 0.0).astype(BF16))
    loads["mask"].wait()
    open_cells = 1.0 - mask[...].astype(F32)
    for i in range(NX):
        row = jnp.zeros((8, 128), F32)
        for j in range(4):
            row = jnp.where(sub // 2 == j, open_cells[i:i + 1, j * 128:j * 128 + 128], row)
        keep[i] = row

    loads["grad"].wait()
    loads["yi"].wait()
    local(0)
    small_start(0)
    bulk_start(1, 0)
    bulk_wait(0)
    small_wait(0)
    owner_upper(0)
    small_start(1)
    bulk_start(1, 1)
    product(t2, m_r, m_r, 1)
    product(t4, t2, t2, 2)
    small_wait(1)
    offset = og[0, 12:24]
    for q in range(12):
        offset += st_q.reshape(12, 12, 8, 128)[:, q] * ef[0, q]
    og[0, 12:24] = offset
    small_start(2)
    bulk_start(1, 2)
    bulk_start(2, 0)
    bulk_wait(1)
    small_wait(2)
    owner_lower(0, None)
    small_start(3)
    bulk_start(2, 1)
    product(s2, n_r, n_r, 7)
    product(s4, s2, s2, 6)
    small_wait(3)
    for i in (7, 0):
        psi[1, i + 1] = solved(0, i)
    halo_start(1, (0, 1))
    for i in range(1, 7):
        psi[1, i + 1] = solved(0, i)
    halo_start(1, (2, 3))
    bulk_start(2, 2)
    local(1)
    small_start(4)
    bulk_wait(2)
    small_wait(4)
    owner_lower(1, owner_upper(1))
    small_start(5)
    loads["sens"].wait()
    factor = []
    for c in range(2):
        value = 0.0
        for n in range(8):
            value = value + jnp.where(ci[c] == n, wt[n], 0.0)
        factor.append(value)
    weight = jnp.where(sub % 2 == 0, factor[0], factor[1])
    small_wait(5)
    tiles = [[jnp.zeros((8, 128), F32) for _ in range(4)] for _ in range(3)]
    for i in range(NX):
        new = solved(1, i)
        psi_o[i] = new
        new = new * weight
        for m in range(3):
            total = jnp.zeros((8, 128), F32)
            for v in range(6):
                total += new[v] * sens[i, m, v]
            total += pltpu.roll(total, 7, 0)
            for j in range(4):
                shift = (i - 2 * j) % 8
                turned = pltpu.roll(total, shift, 0) if shift else total
                tiles[m][j] = jnp.where(sub == i, turned, tiles[m][j])
    for m in range(3):
        for j in range(4):
            part_o[m, :, j * 128:j * 128 + 128] = tiles[m][j]
    across = pltpu.make_async_remote_copy(
        src_ref=part_o, dst_ref=part_r, send_sem=sum_sem.at[0], recv_sem=sum_sem.at[1],
        device_id={"cond": 1 - cond}, device_id_type=MESH)
    across.start()
    for n in range(3):
        bulk_drain(n)
    for it in range(2):
        halo_drain(it)
    for n in range(6):
        small_drain(n)
    across.wait()
    ms_o[...] = part_o[...] + part_r[...]


def hand_over(psi_i, sens_i, psi_o, sens_o, sem):
    copies = [pltpu.make_async_copy(psi_i, psi_o, sem.at[0]), pltpu.make_async_copy(sens_i, sens_o, sem.at[1])]
    for copy in copies:
        copy.start()
    for copy in copies:
        copy.wait()


def on_device(
    psi_old, objective_grad, near_upper, far_upper, inverse_diag, near_lower, far_lower,
    y_inverse, z_inverse, sens_terms, wall_mask, cond_index, weight_table,
):
    cell = (8, 6, 8, 128)
    block = (8, 6, 6, 8, 128)
    matrix = (12, 12, 8, 128)
    vm = lambda *shape: pltpu.VMEM(shape, F32)
    dma = pltpu.SemaphoreType.DMA
    far = pl.BlockSpec(memory_space=pl.ANY)
    scalars = pl.BlockSpec(memory_space=pltpu.SMEM)
    near = pl.BlockSpec(memory_space=pltpu.VMEM)
    psi, sens = pl.pallas_call(
        kernel,
        name="adjoint",
        out_shape=(pltpu.VMEM(cell, F32), pltpu.VMEM((3, 8, 512), F32)),
        in_specs=[far] * 11 + [scalars] * 2,
        out_specs=(near, near),
        scratch_shapes=[
            vm(*cell), vm(*block), vm(*block), vm(*block), vm(*block), vm(*block), vm(*block),
            vm(2, 6, 32, 32), vm(8, 3, 6, 8, 128), pltpu.VMEM((8, 512), jnp.int32),
            vm(2, 10, 6, 8, 128), vm(16, 2, 6, 8, 128), vm(8, 8, 128), pltpu.VMEM((6, 256, 256), BF16),
            vm(6, 8, 8, 128), vm(6, 8, 8, 128), vm(*cell), vm(*cell),
            vm(2, 24, 8, 128), vm(2, 24, 8, 128), vm(2, 24, 8, 128), vm(2, 24, 8, 128),
            vm(10, 6, 12, 8, 128), vm(8, 6, 12, 8, 128), vm(8, 6, 12, 8, 128),
            vm(2, 6, 12, 8, 128), vm(2, 6, 12, 8, 128), vm(6, 12, 8, 128),
            vm(*matrix), vm(*matrix), vm(*matrix), vm(*matrix), vm(*matrix), vm(*matrix), vm(*matrix), vm(*matrix),
            vm(3, 8, 512), vm(3, 8, 512),
            dma((11,)), dma((7, 8)), dma((7, 8)), dma((6, 8)), dma((6, 8)), dma((2, 4)), dma((2, 4)),
            dma((9,)), dma((2,)),
        ],
        compiler_params=pltpu.CompilerParams(
            collective_id=0, has_side_effects=True, vmem_limit_bytes=58 * 2**20),
        cost_estimate=pl.CostEstimate(flops=10**8, bytes_accessed=9 * 10**6, transcendentals=0),
    )(
        pack(psi_old), pack(objective_grad), pack(near_upper), pack(far_upper), pack(inverse_diag),
        pack(near_lower), pack(far_lower), pack(y_inverse), z_inverse, pack(sens_terms),
        wall_mask, cond_index, weight_table,
    )
    psi, sens = pl.pallas_call(
        hand_over,
        name="hand_over",
        out_shape=(jax.ShapeDtypeStruct(cell, F32), jax.ShapeDtypeStruct((3, 8, 512), F32)),
        in_specs=[far, far],
        out_specs=(far, far),
        scratch_shapes=[dma((2,))],
    )(pltpu.with_memory_space_constraint(psi, pltpu.VMEM), pltpu.with_memory_space_constraint(sens, pltpu.VMEM))
    return unpack(psi), jnp.transpose(sens, (1, 0, 2))


def solution(mesh):
    cell = P("gx", "cond", None, "gy")
    block = P("gx", "cond", None, None, "gy")
    placed = (
        cell, cell, block, block, block, block, block, block,
        P("cond", None, None, None), block, P("gx", "gy"), P("cond"), P(),
    )
    return jax.shard_map(
        on_device, mesh=mesh, in_specs=placed, out_specs=(cell, P("gx", None, "gy")), check_vma=False)
```

```python
import functools

import jax
import jax.numpy as jnp
from jax import lax
from jax.experimental import pallas as pl
from jax.experimental.pallas import tpu as pltpu
from jax.sharding import PartitionSpec as P

MESH = pl.DeviceIdType.MESH
F32 = jnp.float32
BF16 = jnp.bfloat16
NX = 8
ORDER = (4, 3, 5, 2, 6, 1, 7)


def pack(x):
    n = x.ndim
    y = jnp.transpose(x, (0,) + tuple(range(2, n - 1)) + (1, n - 1))
    s = y.shape[:-2]
    y = jnp.swapaxes(y.reshape(s + (2, 4, 128)), -3, -2)
    return y.reshape(s + (8, 128))


def unpack(y):
    s = y.shape[:-2]
    y = jnp.swapaxes(y.reshape(s + (4, 2, 128)), -3, -2).reshape(s + (2, 512))
    n = y.ndim
    return jnp.transpose(y, (0, n - 2) + tuple(range(1, n - 2)) + (n - 1,))


def kernel(
    psi_h, grad_h, nu_h, fu_h, inv_h, nl_h, fl_h, yi_h, zi_h, sens_h, mask_h, ci, wt,
    psi_o, ms_o,
    grad, nu, fu, inv, nl, fl, yi, zi, sens, mask,
    psi, hj, keep, weights, xs, zs, up, p0, og, ogr, own, ef,
    resp, pr_e, pr_f, st_n, st_q, diff, m_r, n_r, q_r, t2, t4, s2, s4, rolled, part_o, part_r,
    load_sem, bulk_s, bulk_r, small_s, small_r, halo_s, halo_r, own_sem, sum_sem,
):
    k = lax.axis_index("gx")
    g = lax.axis_index("gy")
    cond = lax.axis_index("cond")
    last_g = lax.axis_size("gy") - 1
    sub = lax.broadcasted_iota(jnp.int32, (8, 128), 0)
    lane = lax.broadcasted_iota(jnp.int32, (8, 128), 1)

    loads = {}
    for n, (name, src, dst) in enumerate((
        ("nu", nu_h, nu), ("fu", fu_h, fu), ("psi", psi_h, psi.at[0, 1:9]), ("inv", inv_h, inv),
        ("nl", nl_h, nl), ("fl", fl_h, fl), ("zi", zi_h, zi), ("grad", grad_h, grad),
        ("yi", yi_h, yi), ("mask", mask_h, mask), ("sens", sens_h, sens),
    )):
        loads[name] = pltpu.make_async_copy(src, dst, load_sem.at[n])
        if n < 3:
            loads[name].start()

    zero = jnp.zeros((8, 128), F32)
    one = jnp.ones((8, 128), F32)
    for it in range(2):
        psi[it, 0] = jnp.zeros((6, 8, 128), F32)
        psi[it, 9] = jnp.zeros((6, 8, 128), F32)

    def clear(i, _):
        hj[i] = jnp.zeros((2, 6, 8, 128), F32)
        return 0

    lax.fori_loop(0, 16, clear, 0)

    def clear_matrix(i, _):
        m_r[i] = jnp.zeros((12, 8, 128), F32)
        n_r[i] = jnp.zeros((12, 8, 128), F32)
        q_r[i] = jnp.zeros((12, 8, 128), F32)
        return 0

    lax.fori_loop(0, 12, clear_matrix, 0)

    barrier = pltpu.get_barrier_semaphore()
    for d in range(1, NX):
        pl.semaphore_signal(barrier, inc=1, device_id={"gx": lax.rem(k + d, NX)}, device_id_type=MESH)
    pl.semaphore_signal(barrier, inc=1, device_id={"cond": 1 - cond}, device_id_type=MESH)

    @pl.when(g > 0)
    def _():
        pl.semaphore_signal(barrier, inc=1, device_id={"gy": g - 1}, device_id_type=MESH)

    @pl.when(g < last_g)
    def _():
        pl.semaphore_signal(barrier, inc=1, device_id={"gy": g + 1}, device_id_type=MESH)

    def halo_copy(it, n):
        if n == 0:
            src, dst, to = psi.at[it, 8], psi.at[it, 0], {"gx": lax.rem(k + 1, NX)}
        elif n == 1:
            src, dst, to = psi.at[it, 1], psi.at[it, 9], {"gx": lax.rem(k + NX - 1, NX)}
        elif n == 2:
            src, dst, to = psi.at[it, 1:9, :, 6:8], hj.at[pl.ds(it * 8, 8), 0, :, 0:2], {"gy": lax.rem(g + 1, last_g + 1)}
        else:
            src, dst, to = psi.at[it, 1:9, :, 0:2], hj.at[pl.ds(it * 8, 8), 1, :, 6:8], {"gy": lax.rem(g + last_g, last_g + 1)}
        return pltpu.make_async_remote_copy(
            src_ref=src, dst_ref=dst, send_sem=halo_s.at[it, n], recv_sem=halo_r.at[it, n],
            device_id=to, device_id_type=MESH)

    sends = (k < NX - 1, k > 0, g < last_g, g > 0)
    takes = (k > 0, k < NX - 1, g > 0, g < last_g)

    def halo_start(it, which):
        for n in which:
            @pl.when(sends[n])
            def _(n=n):
                halo_copy(it, n).start()

    def halo_wait(it):
        for n in range(4):
            @pl.when(takes[n])
            def _(n=n):
                halo_copy(it, n).wait_recv()

    def halo_drain(it):
        for n in range(4):
            @pl.when(sends[n])
            def _(n=n):
                halo_copy(it, n).wait_send()

    bulk = (
        (resp.reshape(720, 8, 128).at[576:720], m_r, lambda x: (x > 0) & (x < NX - 1), 1, (0, 144), 0),
        (st_n.reshape(144, 8, 128), n_r, lambda x: (x > 0) & (x < NX - 1), -1, (0, 48, 96, 144), 1),
        (st_q.reshape(144, 8, 128), q_r, lambda x: x > 0, -1, (0, 32, 96, 144), 4),
    )

    def bulk_copy(n, d, source, part):
        src, dst, _, move, cuts, first = bulk[n]
        to = lax.rem(source + d, NX)
        row = lax.rem(source + NX + move, NX)
        span = slice(cuts[part], cuts[part + 1])
        return pltpu.make_async_remote_copy(
            src_ref=src.at[span, to], dst_ref=dst.reshape(144, 8, 128).at[span, row],
            send_sem=bulk_s.at[first + part, d], recv_sem=bulk_r.at[first + part, d],
            device_id={"gx": to}, device_id_type=MESH)

    def bulk_own(n):
        src, dst, _, move, _, _ = bulk[n]
        row = lax.rem(k + NX + move, NX)
        return pltpu.make_async_copy(src.at[:, k], dst.reshape(144, 8, 128).at[:, row], own_sem.at[n])

    def bulk_start(n, part=0):
        @pl.when(bulk[n][2](k))
        def _():
            for d in ORDER:
                bulk_copy(n, d, k, part).start()
            if part == 0:
                bulk_own(n).start()

    def bulk_wait(n):
        for part in range(len(bulk[n][4]) - 1):
            for d in ORDER:
                source = lax.rem(k + NX - d, NX)

                @pl.when(bulk[n][2](source))
                def _(d=d, source=source, part=part):
                    bulk_copy(n, d, source, part).wait_recv()

        @pl.when(bulk[n][2](k))
        def _():
            bulk_own(n).wait()

    def bulk_drain(n):
        @pl.when(bulk[n][2](k))
        def _():
            for part in range(len(bulk[n][4]) - 1):
                for d in ORDER:
                    bulk_copy(n, d, k, part).wait_send()

    small = ((0, 0, 0, 12), (0, 1, 0, 12), (0, 0, 12, 24), (0, 1, 12, 24), (1, 0, 0, 24), (1, 1, 0, 24))

    def small_copy(n, d, source):
        it, back, first, end = small[n]
        src, dst = (own, ef) if back else (og, ogr)
        to = lax.rem(source + d, NX)
        return pltpu.make_async_remote_copy(
            src_ref=src.at[it, first:end, to], dst_ref=dst.at[it, first:end, source],
            send_sem=small_s.at[n, d], recv_sem=small_r.at[n, d],
            device_id={"gx": to}, device_id_type=MESH)

    def small_own(n):
        it, back, first, end = small[n]
        src, dst = (own, ef) if back else (og, ogr)
        return pltpu.make_async_copy(src.at[it, first:end, k], dst.at[it, first:end, k], own_sem.at[3 + n])

    def small_start(n):
        for d in ORDER:
            small_copy(n, d, k).start()
        small_own(n).start()

    def small_wait(n):
        for d in ORDER:
            small_copy(n, d, lax.rem(k + NX - d, NX)).wait_recv()
        small_own(n).wait()

    def small_drain(n):
        for d in ORDER:
            small_copy(n, d, k).wait_send()

    def upper_response(i, _):
        for w in range(0, 6, 2):
            acc = jnp.zeros((2, 12, 8, 128), F32)
            for v in range(6):
                acc += nu[i, w:w + 2, v][:, None] * resp[i + 1, v][None]
                acc += fu[i, w:w + 2, v][:, None] * resp[i, v][None]
            resp[i + 2, w:w + 2] = -acc
        return 0

    def lower_response(state, out, with_upper, t, _):
        i = NX - 1 - t
        for v in range(6):
            if with_upper:
                diff[v] = resp[i + 2, v] - state[0, v]
            else:
                diff[v] = -state[0, v]
        for w in range(0, 6, 2):
            acc = jnp.zeros((2, 12, 8, 128), F32)
            for v in range(6):
                acc += inv[i, v, w:w + 2][:, None] * diff[v][None]
            out[i, w:w + 2] = acc
        for w in range(0, 6, 2):
            near = state[1, w:w + 2]
            far = jnp.zeros((2, 12, 8, 128), F32)
            for v in range(6):
                p = out[i, v][None]
                near += nl[i, v, w:w + 2][:, None] * p
                far += fl[i, v, w:w + 2][:, None] * p
            state[0, w:w + 2] = near
            state[1, w:w + 2] = far
        return 0

    def local(it):
        halo_wait(it)
        for i in range(NX):
            here = psi[it, i + 1]
            down = pltpu.roll(here, 2, 1)
            down = jnp.where(sub < 2, hj[it * 8 + i, 0], down)
            down = pltpu.roll(jnp.where(lane >= 96, down, here), 32, 2)
            above = pltpu.roll(here, 6, 1)
            above = jnp.where(sub >= 6, hj[it * 8 + i, 1], above)
            above = pltpu.roll(jnp.where(lane < 32, above, here), 96, 2)
            beside = psi[it, i] + psi[it, i + 2] + down + above
            xs[:, i] = grad[i] + 0.5 * beside - 2.0 * here
        for v in range(6):
            x = xs[v].reshape(64, 128)
            hi = x.astype(BF16)
            lo = (x - hi.astype(F32)).astype(BF16)
            both = jnp.concatenate(
                [jnp.concatenate([hi, hi], axis=1), jnp.concatenate([lo, lo], axis=1)], axis=0)
            r = jnp.dot(both, weights[v], preferred_element_type=F32)
            r = (r[:64] + r[64:]).reshape(8, 8, 256)
            zs[v] = jnp.where(sub % 2 == 0, r[:, :, :128], r[:, :, 128:])
        last = jnp.zeros((6, 8, 128), F32)
        before = jnp.zeros((6, 8, 128), F32)
        for i in range(NX):
            now = jnp.zeros((6, 8, 128), F32)
            for v in range(6):
                now += yi[i, v] * zs[v, i]
            for v in range(6):
                now -= fu[i, :, v] * before[v]
            for v in range(6):
                now -= nu[i, :, v] * last[v]
            up[i] = now
            last, before = now, last
        og[it, 0:6] = before
        og[it, 6:12] = last
        pending = jnp.zeros((6, 8, 128), F32)
        partial = jnp.zeros((6, 8, 128), F32)
        for i in range(NX - 1, -1, -1):
            d = up[i] - pending
            p = jnp.zeros((6, 8, 128), F32)
            for v in range(6):
                p += inv[i, v] * d[v]
            p0[i] = p
            pending = partial
            partial = jnp.zeros((6, 8, 128), F32)
            for v in range(6):
                pending += nl[i, v] * p[v]
                partial += fl[i, v] * p[v]
        og[it, 12:18] = pending
        og[it, 18:24] = partial

    def product(dst, a, b, shift):
        def turn(q, _):
            rolled[q] = pltpu.roll(b[q], shift, 1)
            return 0

        lax.fori_loop(0, 12, turn, 0)

        def rows(m, _):
            acc = jnp.zeros((2, 12, 8, 128), F32)
            for q in range(12):
                acc += a[pl.ds(2 * m, 2), q][:, None] * rolled[q][None]
            dst[pl.ds(2 * m, 2)] = acc
            return 0

        lax.fori_loop(0, 6, rows, 0)

    def apply(x, a, by, shift):
        turned = pltpu.roll(by, shift, 1)
        for q in range(12):
            x = x + a[:, q] * turned[q]
        return x

    def steps(x, a, shift):
        return lax.fori_loop(0, NX - 2, lambda _, y: apply(x, a, y, shift), x)

    def owner_upper(it):
        u = jnp.where(sub == 0, 0.0, pltpu.roll(ogr[it, 0:12], 1, 1))
        if it == 0:
            u = steps(u, m_r, 1)
        else:
            u = apply(u, m_r, u, 1)
            u = apply(u, t2, u, 2)
            u = apply(u, t4, u, 4)
        own[it, 0:12] = u
        return u

    def owner_lower(it, u):
        w = jnp.where(sub == 7, 0.0, pltpu.roll(ogr[it, 12:24], 7, 1))
        if it == 0:
            w = steps(w, n_r, 7)
        else:
            w = apply(w, q_r, u, 7)
            w = apply(w, n_r, w, 7)
            w = apply(w, s2, w, 6)
            w = apply(w, s4, w, 4)
        own[it, 12:24] = w

    def solved(it, i):
        p = p0[i]
        for q in range(12):
            p += pr_e[i, :, q] * ef[it, q]
        for q in range(12):
            p += pr_f[i, :, q] * ef[it, 12 + q]
        return (psi[it, i + 1] + 0.05 * p) * keep[i]

    for s in range(2):
        for v in range(6):
            for q in range(12):
                unit = one if q == 6 * s + v else zero
                resp[s, v, q] = unit
                st_n[s, v, q] = unit
                st_q[s, v, q] = zero

    loads["nu"].wait()
    loads["fu"].wait()
    for name in ("inv", "nl", "fl", "zi", "grad", "yi", "mask", "sens"):
        loads[name].start()
    lax.fori_loop(0, NX, upper_response, 0)
    loads["psi"].wait()
    neighbours = jnp.where(g > 0, 1, 0) + jnp.where(g < last_g, 1, 0)
    pl.semaphore_wait(barrier, NX + neighbours)
    halo_start(0, range(4))
    bulk_start(0)
    loads["inv"].wait()
    loads["nl"].wait()
    loads["fl"].wait()
    lax.fori_loop(0, NX, functools.partial(lower_response, st_n, pr_f, False), 0)
    lax.fori_loop(0, NX, functools.partial(lower_response, st_q, pr_e, True), 0)

    loads["zi"].wait()
    z = zi[...].reshape(2 * 6 * 32, 32)
    z_hi = z.astype(BF16)
    z_lo = (z - z_hi.astype(F32)).astype(BF16)
    spread = (
        lax.broadcasted_iota(jnp.int32, (32, 128), 1) % 32 == lax.broadcasted_iota(jnp.int32, (32, 128), 0)
    ).astype(F32).astype(BF16)
    lane32 = lax.broadcasted_iota(jnp.int32, (32, 128), 1) // 32
    for half, part in enumerate((z_hi, z_lo)):
        tiled = jnp.dot(part, spread, preferred_element_type=F32)
        for c in range(2):
            for v in range(6):
                at = (c * 6 + v) * 32
                rows = tiled[at:at + 32]
                for b in range(4):
                    weights[v, half * 128 + b * 32:half * 128 + b * 32 + 32, c * 128:c * 128 + 128] = (
                        jnp.where(lane32 == b, rows, 0.0).astype(BF16))
    loads["mask"].wait()
    open_cells = 1.0 - mask[...].astype(F32)
    for i in range(NX):
        row = jnp.zeros((8, 128), F32)
        for j in range(4):
            row = jnp.where(sub // 2 == j, open_cells[i:i + 1, j * 128:j * 128 + 128], row)
        keep[i] = row

    loads["grad"].wait()
    loads["yi"].wait()
    local(0)
    small_start(0)
    bulk_start(1, 0)
    bulk_wait(0)
    small_wait(0)
    owner_upper(0)
    small_start(1)
    bulk_start(1, 1)
    product(t2, m_r, m_r, 1)
    product(t4, t2, t2, 2)
    small_wait(1)
    offset = og[0, 12:24]
    for q in range(12):
        offset += st_q.reshape(12, 12, 8, 128)[:, q] * ef[0, q]
    og[0, 12:24] = offset
    small_start(2)
    bulk_start(1, 2)
    bulk_start(2, 0)
    bulk_wait(1)
    small_wait(2)
    owner_lower(0, None)
    small_start(3)
    bulk_start(2, 1)
    product(s2, n_r, n_r, 7)
    product(s4, s2, s2, 6)
    small_wait(3)
    for i in (7, 0):
        psi[1, i + 1] = solved(0, i)
    halo_start(1, (0, 1))
    for i in range(1, 7):
        psi[1, i + 1] = solved(0, i)
    halo_start(1, (2, 3))
    bulk_start(2, 2)
    local(1)
    small_start(4)
    bulk_wait(2)
    small_wait(4)
    owner_lower(1, owner_upper(1))
    small_start(5)
    loads["sens"].wait()
    factor = []
    for c in range(2):
        value = 0.0
        for n in range(8):
            value = value + jnp.where(ci[c] == n, wt[n], 0.0)
        factor.append(value)
    weight = jnp.where(sub % 2 == 0, factor[0], factor[1])
    small_wait(5)
    tiles = [[jnp.zeros((8, 128), F32) for _ in range(4)] for _ in range(3)]
    for i in range(NX):
        new = solved(1, i)
        psi_o[i] = new
        new = new * weight
        for m in range(3):
            total = jnp.zeros((8, 128), F32)
            for v in range(6):
                total += new[v] * sens[i, m, v]
            total += pltpu.roll(total, 7, 0)
            for j in range(4):
                shift = (i - 2 * j) % 8
                turned = pltpu.roll(total, shift, 0) if shift else total
                tiles[m][j] = jnp.where(sub == i, turned, tiles[m][j])
    for m in range(3):
        for j in range(4):
            part_o[m, :, j * 128:j * 128 + 128] = tiles[m][j]
    across = pltpu.make_async_remote_copy(
        src_ref=part_o, dst_ref=part_r, send_sem=sum_sem.at[0], recv_sem=sum_sem.at[1],
        device_id={"cond": 1 - cond}, device_id_type=MESH)
    across.start()
    for n in range(3):
        bulk_drain(n)
    for it in range(2):
        halo_drain(it)
    for n in range(6):
        small_drain(n)
    across.wait()
    ms_o[...] = part_o[...] + part_r[...]


def hand_over(psi_i, sens_i, psi_o, sens_o, sem):
    copies = [pltpu.make_async_copy(psi_i, psi_o, sem.at[0]), pltpu.make_async_copy(sens_i, sens_o, sem.at[1])]
    for copy in copies:
        copy.start()
    for copy in copies:
        copy.wait()


def on_device(
    psi_old, objective_grad, near_upper, far_upper, inverse_diag, near_lower, far_lower,
    y_inverse, z_inverse, sens_terms, wall_mask, cond_index, weight_table,
):
    cell = (8, 6, 8, 128)
    block = (8, 6, 6, 8, 128)
    matrix = (12, 12, 8, 128)
    vm = lambda *shape: pltpu.VMEM(shape, F32)
    dma = pltpu.SemaphoreType.DMA
    far = pl.BlockSpec(memory_space=pl.ANY)
    scalars = pl.BlockSpec(memory_space=pltpu.SMEM)
    near = pl.BlockSpec(memory_space=pltpu.VMEM)
    psi, sens = pl.pallas_call(
        kernel,
        name="adjoint",
        out_shape=(pltpu.VMEM(cell, F32), pltpu.VMEM((3, 8, 512), F32)),
        in_specs=[far] * 11 + [scalars] * 2,
        out_specs=(near, near),
        scratch_shapes=[
            vm(*cell), vm(*block), vm(*block), vm(*block), vm(*block), vm(*block), vm(*block),
            vm(2, 6, 32, 32), vm(8, 3, 6, 8, 128), pltpu.VMEM((8, 512), jnp.int32),
            vm(2, 10, 6, 8, 128), vm(16, 2, 6, 8, 128), vm(8, 8, 128), pltpu.VMEM((6, 256, 256), BF16),
            vm(6, 8, 8, 128), vm(6, 8, 8, 128), vm(*cell), vm(*cell),
            vm(2, 24, 8, 128), vm(2, 24, 8, 128), vm(2, 24, 8, 128), vm(2, 24, 8, 128),
            vm(10, 6, 12, 8, 128), vm(8, 6, 12, 8, 128), vm(8, 6, 12, 8, 128),
            vm(2, 6, 12, 8, 128), vm(2, 6, 12, 8, 128), vm(6, 12, 8, 128),
            vm(*matrix), vm(*matrix), vm(*matrix), vm(*matrix), vm(*matrix), vm(*matrix), vm(*matrix), vm(*matrix),
            vm(3, 8, 512), vm(3, 8, 512),
            dma((11,)), dma((7, 8)), dma((7, 8)), dma((6, 8)), dma((6, 8)), dma((2, 4)), dma((2, 4)),
            dma((9,)), dma((2,)),
        ],
        compiler_params=pltpu.CompilerParams(
            collective_id=0, has_side_effects=True, vmem_limit_bytes=58 * 2**20),
        cost_estimate=pl.CostEstimate(flops=10**8, bytes_accessed=9 * 10**6, transcendentals=0),
    )(
        pack(psi_old), pack(objective_grad), pack(near_upper), pack(far_upper), pack(inverse_diag),
        pack(near_lower), pack(far_lower), pack(y_inverse), z_inverse, pack(sens_terms),
        wall_mask, cond_index, weight_table,
    )
    psi, sens = pl.pallas_call(
        hand_over,
        name="hand_over",
        out_shape=(jax.ShapeDtypeStruct(cell, F32), jax.ShapeDtypeStruct((3, 8, 512), F32)),
        in_specs=[far, far],
        out_specs=(far, far),
        scratch_shapes=[dma((2,))],
    )(pltpu.with_memory_space_constraint(psi, pltpu.VMEM), pltpu.with_memory_space_constraint(sens, pltpu.VMEM))
    return unpack(psi), jnp.transpose(sens, (1, 0, 2))


def solution(mesh):
    cell = P("gx", "cond", None, "gy")
    block = P("gx", "cond", None, None, "gy")
    placed = (
        cell, cell, block, block, block, block, block, block,
        P("cond", None, None, None), block, P("gx", "gy"), P("cond"), P(),
    )
    return jax.shard_map(
        on_device, mesh=mesh, in_specs=placed, out_specs=(cell, P("gx", None, "gy")), check_vma=False)
```
